32 devices in a mesh: fsdp: 8 (over z, core), ctx: 2 (over y), tp: 2 (over x).
Axes of the slice: x: 2, y: 2, z: 4, core: 2. Of those that a mesh axis runs over, the one named last changes fastest.
Arguments:
- hidden_in: bfloat16 [8, 1024, 1024], P('fsdp', 'ctx'), may hold values from -6 to 6
- segment_ids: int32 [8, 1024], P('fsdp'), may hold values from 0 to 4, as said below
- expert_ids: int32 [8, 1024, 8], P('fsdp', 'ctx'), may hold values from 0 to 31, all different within a row; in each aligned block of 512 rows (0 to 511, 512 to 1023, ..., all dimensions but the last counted through in order) at most 256 rows name the same one
- norm1_gain: bfloat16 [1024], P('fsdp'), may hold values from 0.5 to 1.5
- w_query: bfloat16 [1024, 1024], P('fsdp', 'tp'), may hold values from -0.1875 to 0.1875
- w_key: bfloat16 [1024, 512], P('fsdp', 'tp'), may hold values from -0.1875 to 0.1875
- w_value: bfloat16 [1024, 512], P('fsdp', 'tp'), may hold values from -0.1875 to 0.1875
- w_output: bfloat16 [1024, 1024], P('tp', 'fsdp'), may hold values from -1.5 to 1.5
- norm2_gain: bfloat16 [1024], P('fsdp'), may hold values from 0.5 to 1.5
- w_router: bfloat16 [1024, 32], P('fsdp'), may hold values from -0.09375 to 0.09375
- w_gate: bfloat16 [32, 1024, 512], P(None, 'fsdp', 'tp'), may hold values from -0.1875 to 0.1875
- w_up: bfloat16 [32, 1024, 512], P(None, 'fsdp', 'tp'), may hold values from -0.1875 to 0.1875
- w_down: bfloat16 [32, 512, 1024], P(None, 'tp', 'fsdp'), may hold values from -3 to 3
- cotangent: bfloat16 [8, 1024, 1024], P('fsdp', 'ctx'), may hold values from -6 to 6
Outputs:
- block_out: bfloat16 [8, 1024, 1024], P('fsdp', 'ctx')
- grad_hidden_in: float32 [8, 1024, 1024], P('fsdp', 'ctx')
- grad_norm1_gain: float32 [1024], P('fsdp')
- grad_w_query: float32 [1024, 1024], P('fsdp', 'tp')
- grad_w_key: float32 [1024, 512], P('fsdp', 'tp')
- grad_w_value: float32 [1024, 512], P('fsdp', 'tp')
- grad_w_output: float32 [1024, 1024], P('tp', 'fsdp')
- grad_norm2_gain: float32 [1024], P('fsdp')
- grad_w_router: float32 [1024, 32], P('fsdp')
- grad_w_gate: float32 [32, 1024, 512], P(None, 'fsdp', 'tp')
- grad_w_up: float32 [32, 1024, 512], P(None, 'fsdp', 'tp')
- grad_w_down: float32 [32, 512, 1024], P(None, 'tp', 'fsdp')
The draws below stay inside these ranges and needn't reach their ends.
Inputs may be any that keep to these rules, and one draw needn't show every extreme that they name: `segment_ids`: segment numbers never fall along a row and every row holds all five; in each row document 2 begins within the first 512 positions and ends within the last 512. `expert_ids`: A token names 8 different experts. In each aligned block of 512 tokens of a row (one device's positions of one sequence) no expert is named by more than 256 tokens, and in some block one expert is named by exactly 256.
All inputs are finite; a program needn't handle non-finite values.
Results may differ from the reference program's by a relative error of at most 0.02.
Values may be sent and summed in bfloat16 or wider, within the bound.
A program may use at most 384 MiB of HBM per device.

```python
import math
import jax
import jax.numpy as jnp
import numpy as np
from jax import lax

D = 1024
HQ = 16
HK = 8
HD = 64
E = 32
FF = 512
TOPK = 8
CTX_TOK = 512
LENGTH = 1024
BATCH = 8
CAP = 256


def draw_segment_ids(key, part):
    key = jax.random.fold_in(key, 7)
    split_keys = jax.random.split(key, 4)
    first_end = jax.random.randint(split_keys[0], (BATCH, 1), 2, CTX_TOK)
    first_cut = jax.random.randint(split_keys[1], (BATCH, 1), 1, first_end)
    last_start = jax.random.randint(split_keys[2], (BATCH, 1), LENGTH - CTX_TOK + 1, LENGTH - 1)
    last_cut = jax.random.randint(split_keys[3], (BATCH, 1), last_start + 1, LENGTH)
    index = jnp.arange(LENGTH, dtype=jnp.int32)[None, :]
    marks = (index >= first_cut).astype(jnp.int32) + (index >= first_end).astype(jnp.int32)
    marks = marks + (index >= last_start).astype(jnp.int32) + (index >= last_cut).astype(jnp.int32)
    return marks


def steps_of(rng, dims, cuts, low, top_value):
    def one(position, parts):
        steps = jax.random.uniform(jax.random.fold_in(jax.random.fold_in(rng, 6), position), (parts,), jnp.float32, low / len(cuts), top_value / len(cuts))
        return jnp.repeat(jnp.exp(steps), dims[position] // parts).reshape((-1,) + (1,) * (len(dims) - position - 1))

    level = one(*cuts[0])
    for cut in cuts[1:]:
        level = level * one(*cut)
    return level


def shared_out(stream_key, own, number, rows, number_of, top, most, slope):
    ranking = jax.random.permutation(stream_key, number_of)
    packed, ordinary = shares(number_of, rows * top, most, slope, True), shares(number_of, rows * top, most, slope, False)
    places = jnp.arange(number_of)

    def named(tallies, offset_by):
        used = int((tallies > 0).sum())
        fixed = max(1, used // 4)
        moved = fixed + (places - fixed + offset_by * (used - fixed)) % max(1, number_of - fixed)
        return jnp.zeros((number_of,), jnp.int32).at[ranking[jnp.where(places < fixed, places, moved)]].set(jnp.asarray(tallies, jnp.int32))

    tallies = jnp.where(number % 4 == 0, named(packed, number // 4), named(ordinary, number - number // 4 - 1))
    mixed = jax.random.permutation(jax.random.fold_in(own, 3), number_of)
    giver, sink = mixed[0:number_of // 2 * 2:2], mixed[1:number_of // 2 * 2:2]
    margin = jnp.minimum(tallies[giver] - 1, most - tallies[sink]) // 2
    margin = jnp.where((giver == ranking[0]) | (sink == ranking[0]) | (tallies[sink] == 0), 0, jnp.maximum(margin, 0))
    moved = jax.random.randint(jax.random.fold_in(own, 4), (number_of // 2,), 0, 1 << 20) % (margin + 1)
    tallies = tallies.at[giver].add(-moved).at[sink].add(moved)
    labels = jnp.searchsorted(jnp.cumsum(tallies), jnp.arange(rows * top), side="right").astype(jnp.int32)
    grid = labels.reshape(top, rows).T
    grid = grid[jax.random.permutation(jax.random.fold_in(own, 1), rows)]
    offset_by = jax.random.randint(jax.random.fold_in(own, 2), (rows, 1), 0, top)
    return jnp.take_along_axis(grid, (jnp.arange(top)[None, :] + offset_by) % top, axis=1)


def shares(number_of, total, reach, skew, full):
    weights = [(1 << 20) // math.isqrt(rank ** skew) + 1 for rank in range(1, number_of + 1)]
    largest = reach if full else min(reach, max(-(-total // number_of), total * weights[0] // sum(weights)))
    least = 1 if total - largest >= number_of - 1 else 0
    counts, spare = [largest] + [least] * (number_of - 1), total - largest - least * (number_of - 1)
    while spare > 0:
        free = [i for i in range(1, number_of) if counts[i] < largest] or [i for i in range(1, number_of) if counts[i] < reach]
        whole, remaining = sum([weights[i] for i in free]), spare
        for i in free:
            more = min(reach - counts[i], max(1, remaining * weights[i] // whole), spare)
            counts[i] = counts[i] + more
            spare = spare - more
    return np.array(counts)


def scatter_about(stream_key, shape, width, reach, cuts=(), held_as=jnp.bfloat16):
    drawn = width * jax.random.normal(stream_key, shape, jnp.float32)
    if cuts:
        drawn = drawn * steps_of(stream_key, shape, cuts, -0.22, 0.18)
    return jnp.clip(drawn, -reach, reach).astype(held_as)


def setup_inputs(seed: int = 0) -> dict:
    key_of = jax.random.split(jax.random.key(seed), 15)
    hidden_in = scatter_about(key_of[0], (BATCH, LENGTH, D), 1.0, 6.0, ((0, 8), (1, 2)))
    segment_ids = draw_segment_ids(jax.random.fold_in(key_of[14], 71), 0)
    expert_ids_keys = jax.random.split(jax.random.fold_in(key_of[2], 1), BATCH * LENGTH // CTX_TOK)
    expert_ids_turns = jax.random.permutation(jax.random.fold_in(key_of[2], 3), BATCH * LENGTH // CTX_TOK)
    expert_ids = jax.vmap(lambda own, number: shared_out(jax.random.fold_in(key_of[2], 2), own, number, CTX_TOK, E, TOPK, CAP, 1))(expert_ids_keys, expert_ids_turns).reshape((BATCH, LENGTH, TOPK))
    norm1_gain = jnp.clip(1.0 + 0.1 * jax.random.normal(key_of[3], (D,), jnp.float32), 0.5, 1.5).astype(jnp.bfloat16)
    w_query = scatter_about(key_of[4], (D, HQ * HD), D ** -0.5, 0.1875, ((0, 8), (1, 2)))
    w_key = scatter_about(key_of[5], (D, HK * HD), D ** -0.5, 0.1875, ((0, 8), (1, 2)))
    w_value = scatter_about(key_of[6], (D, HK * HD), D ** -0.5, 0.1875, ((0, 8), (1, 2)))
    w_output = scatter_about(key_of[7], (HQ * HD, D), (max(HQ * HD // 64, 1)) ** -0.5, 1.5, ((0, 2), (1, 8)))
    norm2_gain = jnp.clip(1.0 + 0.1 * jax.random.normal(key_of[8], (D,), jnp.float32), 0.5, 1.5).astype(jnp.bfloat16)
    w_router = scatter_about(key_of[9], (D, E), (4 * D) ** -0.5, 0.09375, ((0, 8),))
    w_gate = scatter_about(key_of[10], (E, D, FF), D ** -0.5, 0.1875, ((1, 8), (2, 2)))
    w_up = scatter_about(key_of[11], (E, D, FF), D ** -0.5, 0.1875, ((1, 8), (2, 2)))
    w_down = scatter_about(key_of[12], (E, FF, D), (max(FF // 128, 1)) ** -0.5, 3.0, ((1, 2), (2, 8)))
    cotangent = scatter_about(key_of[13], (BATCH, LENGTH, D), 1.0, 6.0, ((0, 8), (1, 2)))
    return {"hidden_in": hidden_in, "segment_ids": segment_ids, "expert_ids": expert_ids, "norm1_gain": norm1_gain, "w_query": w_query, "w_key": w_key, "w_value": w_value, "w_output": w_output, "norm2_gain": norm2_gain, "w_router": w_router, "w_gate": w_gate, "w_up": w_up, "w_down": w_down, "cotangent": cotangent}


epsilon = 1e-05
rope_base = 10000.0
masked_fill = -1e+30
highest = lax.Precision.HIGHEST

@jax.custom_vjp
def low(v):
    return lax.optimization_barrier(v.astype(jnp.bfloat16)).astype(jnp.float32)

@jax.custom_vjp
def low_back(v):
    return v

def low_keep(v):
    return (low(v), None)

def low_pass(kept, grad):
    return (grad,)

def back_keep(v):
    return (v, None)

def back_low(kept, grad):
    return (low(grad),)
low.defvjp(low_keep, low_pass)
low_back.defvjp(back_keep, back_low)

def matmul(left, right):
    return jnp.dot(left, right, precision=highest, preferred_element_type=jnp.float32)

def rms_factor(values):
    return lax.rsqrt(lax.optimization_barrier(jnp.mean(values * values, axis=-1, keepdims=True)) + epsilon)

def doc_positions(segments):
    index = lax.broadcasted_iota(jnp.int32, segments.shape, 1)
    earlier = jnp.concatenate([segments[:, :1], segments[:, :-1]], axis=1)
    starts = jnp.where((segments != earlier) | (index == 0), index, 0)
    return index - lax.cummax(starts, axis=1)

def rotary_tables(positions, head_size):
    half_size = head_size // 2
    exponent = jnp.arange(half_size, dtype=jnp.float32) * (-2.0 / head_size)
    angles = positions.astype(jnp.float32)[..., None] * jnp.power(rope_base, exponent)
    return (jnp.cos(angles), jnp.sin(angles))

def rotate(values, cosine, sine_tab):
    half_size = values.shape[-1] // 2
    first_half = values[..., :half_size]
    second_half = values[..., half_size:]
    cos_wide = cosine[..., None, :]
    sin_wide = sine_tab[..., None, :]
    return jnp.concatenate([first_half * cos_wide - second_half * sin_wide, second_half * cos_wide + first_half * sin_wide], axis=-1)

def attend_row(parts_in):
    queries, keys_rot, values, segments = parts_in
    seq_len = queries.shape[0]
    index = jnp.arange(seq_len, dtype=jnp.int32)
    allowed = (index[None, :] <= index[:, None]) & (segments[None, :] == segments[:, None])
    group_size = queries.shape[1] // keys_rot.shape[1]
    score_scale = HD ** (-0.5)

    def one_head(head_parts):
        query_head, key_head, value_head = head_parts
        scores = low_back(jnp.dot(query_head, key_head.T, precision=highest, preferred_element_type=jnp.float32) * score_scale)
        scores = jnp.where(allowed, scores, masked_fill)
        row_max = lax.optimization_barrier(jnp.max(scores, axis=-1, keepdims=True))
        exp_vals = jnp.exp(scores - row_max)
        weights_p = exp_vals / lax.optimization_barrier(jnp.sum(exp_vals, axis=-1, keepdims=True))
        return jnp.dot(low(weights_p), value_head, precision=highest, preferred_element_type=jnp.float32)
    query_heads = jnp.transpose(queries, (1, 0, 2))
    key_heads = jnp.repeat(jnp.transpose(keys_rot, (1, 0, 2)), group_size, axis=0)
    value_heads = jnp.repeat(jnp.transpose(values, (1, 0, 2)), group_size, axis=0)
    mixture = lax.map(jax.checkpoint(one_head), (query_heads, key_heads, value_heads))
    return jnp.transpose(mixture, (1, 0, 2))

def forward(inputs, gain_one, query_w, key_w, value_w, out_w, gain_two, router_w, gate_w, up_w, down_w, segments, route_ids):
    batch_rows, seq_len, model_width = inputs.shape
    flat_in = inputs.reshape(-1, model_width)
    normed_one = low(flat_in * rms_factor(flat_in) * gain_one)
    query_lin = low_back(matmul(normed_one, query_w))
    key_lin = low_back(matmul(normed_one, key_w))
    values = low(low_back(matmul(normed_one, value_w)))
    cosine, sine_tab = rotary_tables(doc_positions(segments).reshape(-1), HD)
    queries = low(rotate(query_lin.reshape(-1, HQ, HD), cosine, sine_tab))
    keys_rot = low(rotate(key_lin.reshape(-1, HK, HD), cosine, sine_tab))
    mixture = lax.map(jax.checkpoint(attend_row), (queries.reshape(batch_rows, seq_len, HQ, HD), keys_rot.reshape(batch_rows, seq_len, HK, HD), values.reshape(batch_rows, seq_len, HK, HD), segments))
    att_out = low(low_back(mixture.reshape(-1, HQ * HD)))
    resid = flat_in + low_back(matmul(att_out, out_w))
    normed_two = low(resid * rms_factor(resid) * gain_two)
    logits = low_back(matmul(normed_two, router_w))
    shifted = logits - lax.optimization_barrier(jnp.max(logits, axis=-1, keepdims=True))
    exp_vals = jnp.exp(shifted)
    router = exp_vals / lax.optimization_barrier(jnp.sum(exp_vals, axis=-1, keepdims=True))
    chosen = (route_ids.reshape(-1, TOPK)[:, :, None] == jnp.arange(E, dtype=jnp.int32)).astype(jnp.float32)
    gate_vals = lax.optimization_barrier(jnp.sum(chosen * router[:, None, :], axis=-1))
    weighting = lax.optimization_barrier(jnp.sum(gate_vals[:, :, None] * chosen, axis=1))

    def add_expert(totals, expert_parts):
        gate_e, up_e, down_e, weight_e = expert_parts
        gate_pre = low_back(matmul(normed_two, gate_e))
        up_pre = low_back(matmul(normed_two, up_e))
        hidden = low(gate_pre * jax.nn.sigmoid(gate_pre) * up_pre)
        return (totals + weight_e[:, None] * low_back(matmul(hidden, down_e)), None)
    moe_total, unused = lax.scan(jax.checkpoint(add_expert), jnp.zeros_like(resid), (gate_w, up_w, down_w, weighting.T))
    return (resid + moe_total).reshape(batch_rows, seq_len, model_width)

def reference(hidden_in, segment_ids, expert_ids, norm1_gain, w_query, w_key, w_value, w_output, norm2_gain, w_router, w_gate, w_up, w_down, cotangent):
    primals = (hidden_in.astype(jnp.float32), norm1_gain.astype(jnp.float32), w_query.astype(jnp.float32), w_key.astype(jnp.float32), w_value.astype(jnp.float32), w_output.astype(jnp.float32), norm2_gain.astype(jnp.float32), w_router.astype(jnp.float32), w_gate.astype(jnp.float32), w_up.astype(jnp.float32), w_down.astype(jnp.float32))

    def block(inputs, gain_one, query_w, key_w, value_w, out_w, gain_two, router_w, gate_w, up_w, down_w):
        return forward(inputs, gain_one, query_w, key_w, value_w, out_w, gain_two, router_w, gate_w, up_w, down_w, segment_ids, expert_ids)
    result, pullback = jax.vjp(block, *primals)
    gradients = pullback(cotangent.astype(jnp.float32))
    return (result.astype(jnp.bfloat16), gradients[0], gradients[1], gradients[2], gradients[3], gradients[4], gradients[5], gradients[6], gradients[7], gradients[8], gradients[9], gradients[10])
```

```python
import jax
import jax.numpy as jnp
from jax import lax
from jax.sharding import PartitionSpec as P

HD = 64
E = 32
TOPK = 8


epsilon = 1e-05
rope_base = 10000.0
masked_fill = -1e30


def matmul(left, right):
    return jnp.dot(left, right, preferred_element_type=jnp.float32)


def contract_rows(left, right):
    return lax.dot_general(
        left, right, (((0,), (0,)), ((), ())), preferred_element_type=jnp.float32
    )


def contract_cols(left, right):
    return lax.dot_general(
        left, right, (((1,), (1,)), ((), ())), preferred_element_type=jnp.float32
    )


def rms_factor(values):
    return lax.rsqrt(jnp.mean(values * values, axis=-1, keepdims=True) + epsilon)


def doc_positions(segments):
    index = lax.broadcasted_iota(jnp.int32, segments.shape, 1)
    earlier = jnp.concatenate([segments[:, :1], segments[:, :-1]], axis=1)
    starts = jnp.where((segments != earlier) | (index == 0), index, 0)
    return index - lax.cummax(starts, axis=1)


def rotary_tables(positions, head_size):
    half_size = head_size // 2
    exponent = jnp.arange(half_size, dtype=jnp.float32) * (-2.0 / head_size)
    angles = positions.astype(jnp.float32)[..., None] * jnp.power(rope_base, exponent)
    return (jnp.cos(angles), jnp.sin(angles))


def rotate(values, cosine, sine_tab):
    half_size = values.shape[-1] // 2
    first_half = values[..., :half_size]
    second_half = values[..., half_size:]
    cos_wide = cosine[..., None, :]
    sin_wide = sine_tab[..., None, :]
    return jnp.concatenate(
        [
            first_half * cos_wide - second_half * sin_wide,
            second_half * cos_wide + first_half * sin_wide,
        ],
        axis=-1,
    )


def norm_backward(grad_normed, normed, factor, gain):
    scaled = grad_normed * gain
    return factor * (scaled - normed * jnp.mean(scaled * normed, axis=-1, keepdims=True))


def column_pack(shards, groups):
    experts, depth, units = shards.shape
    local = experts // groups
    return (
        shards.reshape(groups, local, depth, units)
        .transpose(0, 2, 1, 3)
        .reshape(groups, depth, local * units)
    )


def column_unpack(packed, units):
    groups, depth, columns = packed.shape
    local = columns // units
    return (
        packed.reshape(groups, depth, local, units)
        .transpose(0, 2, 1, 3)
        .reshape(groups * local, depth, units)
    )


def gather_experts(shards, groups, ctx_count):
    packed = column_pack(shards, groups)
    part = packed.shape[2] // ctx_count
    mine = lax.dynamic_slice_in_dim(packed, lax.axis_index("ctx") * part, part, 2)
    moved = lax.all_to_all(mine, "fsdp", split_axis=0, concat_axis=0, tiled=True)
    return lax.all_gather(moved.reshape(-1, part), "ctx", axis=1, tiled=True)


def return_experts(grad, groups, units):
    summed = lax.psum_scatter(
        grad.astype(jnp.bfloat16), "ctx", scatter_dimension=1, tiled=True
    )
    depth = summed.shape[0] // groups
    moved = lax.all_to_all(
        summed.reshape(groups, depth, -1), "fsdp", split_axis=0, concat_axis=0, tiled=True
    )
    return column_unpack(lax.all_gather(moved, "ctx", axis=2, tiled=True), units)


def router_probs(normed, router_w):
    logits = matmul(normed, router_w)
    exp_logits = jnp.exp(logits - jnp.max(logits, axis=-1, keepdims=True))
    return exp_logits / jnp.sum(exp_logits, axis=-1, keepdims=True)


def body(
    hidden_in,
    segment_ids,
    expert_ids,
    norm1_gain,
    w_query,
    w_key,
    w_value,
    w_output,
    norm2_gain,
    w_router,
    w_gate,
    w_up,
    w_down,
    cotangent,
):
    row_count, ctx_tok, model_width = hidden_in.shape
    tok_count = row_count * ctx_tok
    seq_len = segment_ids.shape[1]
    first_pos = lax.axis_index("ctx") * ctx_tok
    score_scale = HD ** (-0.5)
    groups = lax.axis_size("fsdp")
    ctx_count = lax.axis_size("ctx")
    hidden_units = w_gate.shape[2]
    q_cols, k_cols, o_cols = w_query.shape[1], w_key.shape[1], w_output.shape[0]
    small_at = q_cols + 2 * k_cols + o_cols
    shard_rows = w_query.shape[0]
    packed_w = lax.all_gather(
        jnp.concatenate(
            [
                w_query,
                w_key,
                w_value,
                w_output.T,
                w_router,
                norm1_gain[:, None],
                norm2_gain[:, None],
                jnp.zeros((shard_rows, 128 - E - 2), jnp.bfloat16),
            ],
            axis=1,
        ),
        "fsdp",
        axis=0,
        tiled=True,
    )
    query_w = packed_w[:, :q_cols]
    key_w = packed_w[:, q_cols : q_cols + k_cols]
    value_w = packed_w[:, q_cols + k_cols : q_cols + 2 * k_cols]
    out_wt = packed_w[:, q_cols + 2 * k_cols : small_at]
    router_w = packed_w[:, small_at : small_at + E]
    gain_one = packed_w[:, small_at + E]
    gain_two = packed_w[:, small_at + E + 1]
    token_ids = expert_ids.reshape(tok_count, TOPK)
    route_mask = jnp.sum(
        (token_ids[:, :, None] == jnp.arange(E, dtype=jnp.int32)).astype(jnp.float32), axis=1
    )
    mask_all = lax.all_gather(route_mask.astype(jnp.bfloat16), "fsdp", axis=0, tiled=True)
    grad_all = lax.all_gather(
        cotangent.reshape(tok_count, model_width), "fsdp", axis=0, tiled=True
    )
    down_wt = gather_experts(w_down.transpose(0, 2, 1), groups, ctx_count)
    gate_w = gather_experts(w_gate, groups, ctx_count)
    up_w = gather_experts(w_up, groups, ctx_count)
    inputs = hidden_in.reshape(tok_count, model_width).astype(jnp.float32)
    factor_one = rms_factor(inputs)
    normed_one = inputs * factor_one
    first_in = (normed_one * gain_one.astype(jnp.float32)).astype(jnp.bfloat16)
    query_lin = matmul(first_in, query_w)
    key_lin = matmul(first_in, key_w)
    values = matmul(first_in, value_w).astype(jnp.bfloat16)
    heads_q = query_lin.shape[1] // HD
    heads_k = key_lin.shape[1] // HD
    group_size = heads_q // heads_k
    positions = doc_positions(segment_ids)
    local_pos = lax.dynamic_slice_in_dim(positions, first_pos, ctx_tok, 1).reshape(tok_count)
    cosine, sine_tab = rotary_tables(local_pos, HD)
    queries = rotate(query_lin.reshape(tok_count, heads_q, HD), cosine, sine_tab).astype(
        jnp.bfloat16
    )
    keys_rot = rotate(key_lin.reshape(tok_count, heads_k, HD), cosine, sine_tab).astype(
        jnp.bfloat16
    )
    kv_all = lax.all_gather(
        jnp.concatenate([keys_rot.reshape(tok_count, heads_k * HD), values], axis=1).reshape(
            row_count, ctx_tok, 2 * heads_k * HD
        ),
        "ctx",
        axis=1,
        tiled=True,
    )
    keys_all, values_all = kv_all[..., : heads_k * HD], kv_all[..., heads_k * HD :]
    pair_count = row_count * heads_k
    query_pairs = (
        queries.reshape(row_count, ctx_tok, heads_k, group_size, HD)
        .transpose(0, 2, 3, 1, 4)
        .reshape(pair_count, group_size * ctx_tok, HD)
    )
    key_pairs = (
        keys_all.reshape(row_count, seq_len, heads_k, HD)
        .transpose(0, 2, 1, 3)
        .reshape(pair_count, seq_len, HD)
    )
    value_pairs = (
        values_all.reshape(row_count, seq_len, heads_k, HD)
        .transpose(0, 2, 1, 3)
        .reshape(pair_count, seq_len, HD)
    )
    row_of = jnp.arange(pair_count, dtype=jnp.int32) // heads_k
    key_index = jnp.arange(seq_len, dtype=jnp.int32)
    query_index = jnp.tile(first_pos + jnp.arange(ctx_tok, dtype=jnp.int32), group_size)

    def pair_scores(query_block, key_block, row_pick):
        seg_row = lax.dynamic_index_in_dim(segment_ids, row_pick, 0, keepdims=False)
        seg_query = jnp.tile(lax.dynamic_slice_in_dim(seg_row, first_pos, ctx_tok), group_size)
        allowed = (key_index[None, :] <= query_index[:, None]) & (
            seg_query[:, None] == seg_row[None, :]
        )
        raw_scores = contract_cols(query_block, key_block) * score_scale
        return jnp.where(allowed, raw_scores, masked_fill)

    def forward_pair(parts_in):
        query_block, key_block, value_block, row_pick = parts_in
        scores = pair_scores(query_block, key_block, row_pick)
        row_max = jnp.max(scores, axis=-1, keepdims=True)
        exp_vals = jnp.exp(scores - row_max)
        totals = jnp.sum(exp_vals, axis=-1, keepdims=True)
        weights_p = (exp_vals / totals).astype(jnp.bfloat16)
        return (matmul(weights_p, value_block), (row_max + jnp.log(totals))[:, 0])

    mixture, log_totals = lax.map(forward_pair, (query_pairs, key_pairs, value_pairs, row_of))
    att_out = (
        mixture.reshape(row_count, heads_k, group_size, ctx_tok, HD)
        .transpose(0, 3, 1, 2, 4)
        .reshape(tok_count, heads_q * HD)
        .astype(jnp.bfloat16)
    )
    resid = inputs + lax.psum(
        contract_cols(att_out, out_wt).astype(jnp.bfloat16), "tp"
    ).astype(jnp.float32)
    factor_two = rms_factor(resid)
    normed_two = resid * factor_two
    second_in = (normed_two * gain_two.astype(jnp.float32)).astype(jnp.bfloat16)
    router = router_probs(second_in, router_w)
    normed_all = lax.all_gather(second_in, "fsdp", axis=0, tiled=True)
    columns = gate_w.shape[1]
    column_expert = lax.axis_index("fsdp") * (columns // hidden_units) + (
        jnp.arange(columns, dtype=jnp.int32) // hidden_units
    )
    owner = (jnp.arange(E, dtype=jnp.int32)[:, None] == column_expert[None, :]).astype(
        jnp.float32
    )
    grad_mid = matmul(grad_all, down_wt)
    gates_all = router_probs(normed_all, router_w) * mask_all.astype(jnp.float32)
    gate_cols = jnp.dot(
        gates_all, owner, precision=lax.Precision.HIGHEST, preferred_element_type=jnp.float32
    )
    gate_pre = matmul(normed_all, gate_w)
    up_pre = matmul(normed_all, up_w)
    sigmoid_g = jax.nn.sigmoid(gate_pre)
    activated = gate_pre * sigmoid_g
    hidden = activated * up_pre
    weighted = (hidden * gate_cols).astype(jnp.bfloat16)
    grad_hidden = grad_mid * gate_cols
    grad_gate_pre = (
        grad_hidden * up_pre * sigmoid_g * (1.0 + gate_pre * (1.0 - sigmoid_g))
    ).astype(jnp.bfloat16)
    grad_up_pre = (grad_hidden * activated).astype(jnp.bfloat16)
    gate_grad_all = contract_cols(
        (hidden * grad_mid).astype(jnp.bfloat16), owner.astype(jnp.bfloat16)
    )
    grad_route = (
        lax.psum_scatter(gate_grad_all, "fsdp", scatter_dimension=0, tiled=True) * route_mask
    )
    grad_rows = contract_cols(grad_gate_pre, gate_w) + contract_cols(grad_up_pre, up_w)
    grad_in_part = lax.psum_scatter(
        grad_rows.astype(jnp.bfloat16), "fsdp", scatter_dimension=0, tiled=True
    )
    moe_rows = contract_cols(weighted, down_wt).astype(jnp.bfloat16)
    moe_rows, _ = lax.optimization_barrier((moe_rows, grad_in_part))
    moe_part = lax.psum_scatter(moe_rows, "fsdp", scatter_dimension=0, tiled=True)
    gate_part = return_experts(contract_rows(normed_all, grad_gate_pre), groups, hidden_units)
    up_part = return_experts(contract_rows(normed_all, grad_up_pre), groups, hidden_units)
    down_part = return_experts(
        contract_rows(grad_all, weighted), groups, hidden_units
    ).transpose(0, 2, 1)
    grad_out = cotangent.reshape(tok_count, model_width).astype(jnp.float32)
    grad_logits = (
        router * (grad_route - jnp.sum(router * grad_route, axis=-1, keepdims=True))
    ).astype(jnp.bfloat16)
    grad_router = contract_rows(second_in, grad_logits)
    grad_second = lax.psum(
        (grad_in_part.astype(jnp.float32) + contract_cols(grad_logits, router_w)).astype(
            jnp.bfloat16
        ),
        "tp",
    ).astype(jnp.float32)
    moe_part, _ = lax.optimization_barrier((moe_part, grad_second))
    moe_total = lax.psum(moe_part, "tp").astype(jnp.float32)
    block_out = (resid + moe_total).astype(jnp.bfloat16).reshape(row_count, ctx_tok, model_width)
    grad_gain_two = jnp.sum(grad_second * normed_two, axis=0)
    grad_resid = grad_out + norm_backward(
        grad_second, normed_two, factor_two, gain_two.astype(jnp.float32)
    )
    grad_att = grad_resid.astype(jnp.bfloat16)
    grad_out_wt = contract_rows(grad_att, att_out)
    grad_att_out = matmul(grad_att, out_wt).astype(jnp.bfloat16)
    grad_out_pairs = (
        grad_att_out.reshape(row_count, ctx_tok, heads_k, group_size, HD)
        .transpose(0, 2, 3, 1, 4)
        .reshape(pair_count, group_size * ctx_tok, HD)
    )

    def backward_pair(parts_in):
        query_block, key_block, value_block, grad_block, log_row, row_pick = parts_in
        scores = pair_scores(query_block, key_block, row_pick)
        weights_p = jnp.exp(scores - log_row[:, None])
        grad_p = contract_cols(grad_block, value_block)
        grad_v = contract_rows(weights_p.astype(jnp.bfloat16), grad_block)
        grad_s = (
            weights_p * (grad_p - jnp.sum(weights_p * grad_p, axis=-1, keepdims=True))
        ).astype(jnp.bfloat16)
        grad_q = matmul(grad_s, key_block) * score_scale
        grad_k = contract_rows(grad_s, query_block) * score_scale
        return (grad_q, grad_k, grad_v)

    grad_q_pairs, grad_k_pairs, grad_v_pairs = lax.map(
        backward_pair, (query_pairs, key_pairs, value_pairs, grad_out_pairs, log_totals, row_of)
    )
    grad_k_rows = (
        grad_k_pairs.reshape(row_count, heads_k, seq_len, HD)
        .transpose(0, 2, 1, 3)
        .reshape(row_count, seq_len, heads_k * HD)
    )
    grad_v_rows = (
        grad_v_pairs.reshape(row_count, heads_k, seq_len, HD)
        .transpose(0, 2, 1, 3)
        .reshape(row_count, seq_len, heads_k * HD)
    )
    own_kv = lax.psum_scatter(
        jnp.concatenate([grad_k_rows, grad_v_rows], axis=2).astype(jnp.bfloat16),
        "ctx",
        scatter_dimension=1,
        tiled=True,
    ).astype(jnp.float32)
    own_k, own_v = own_kv[..., : heads_k * HD], own_kv[..., heads_k * HD :]
    grad_q_rot = (
        grad_q_pairs.reshape(row_count, heads_k, group_size, ctx_tok, HD)
        .transpose(0, 3, 1, 2, 4)
        .reshape(tok_count, heads_q, HD)
    )
    grad_query_lin = (
        rotate(grad_q_rot, cosine, -sine_tab).reshape(tok_count, heads_q * HD).astype(jnp.bfloat16)
    )
    grad_key_lin = (
        rotate(own_k.reshape(tok_count, heads_k, HD), cosine, -sine_tab)
        .reshape(tok_count, heads_k * HD)
        .astype(jnp.bfloat16)
    )
    grad_value_lin = own_v.reshape(tok_count, heads_k * HD).astype(jnp.bfloat16)
    grad_qkv = contract_rows(
        first_in, jnp.concatenate([grad_query_lin, grad_key_lin, grad_value_lin], axis=1)
    )
    grad_first_part = (
        contract_cols(grad_query_lin, query_w)
        + contract_cols(grad_key_lin, key_w)
        + contract_cols(grad_value_lin, value_w)
    )
    grad_first_part, _ = lax.optimization_barrier((grad_first_part, moe_total))
    grad_first = lax.psum(grad_first_part.astype(jnp.bfloat16), "tp").astype(jnp.float32)
    grad_input = grad_resid + norm_backward(
        grad_first, normed_one, factor_one, gain_one.astype(jnp.float32)
    )
    grad_gain_one = jnp.sum(grad_first_part * normed_one, axis=0)
    counted = (lax.axis_index("tp") == 0).astype(jnp.float32)
    dense = lax.psum_scatter(
        jnp.concatenate(
            [
                grad_qkv.astype(jnp.bfloat16),
                grad_out_wt.astype(jnp.bfloat16),
                grad_router.astype(jnp.bfloat16),
                grad_gain_one.astype(jnp.bfloat16)[:, None],
                (grad_gain_two * counted).astype(jnp.bfloat16)[:, None],
                jnp.zeros((model_width, 128 - E - 2), jnp.bfloat16),
            ],
            axis=1,
        ),
        "fsdp",
        scatter_dimension=0,
        tiled=True,
    )
    large = lax.psum(dense[:, :small_at], "ctx").astype(jnp.float32)
    small = lax.psum(dense[:, small_at:], ("ctx", "tp")).astype(jnp.float32)
    return (
        block_out,
        grad_input.reshape(row_count, ctx_tok, model_width),
        small[:, E],
        large[:, :q_cols],
        large[:, q_cols : q_cols + k_cols],
        large[:, q_cols + k_cols : q_cols + 2 * k_cols],
        large[:, q_cols + 2 * k_cols :].T,
        small[:, E + 1],
        small[:, :E],
        gate_part.astype(jnp.float32),
        up_part.astype(jnp.float32),
        down_part.astype(jnp.float32),
    )


def solution(mesh):
    placed = (
        P("fsdp", "ctx", None),
        P("fsdp", None),
        P("fsdp", "ctx", None),
        P("fsdp"),
        P("fsdp", "tp"),
        P("fsdp", "tp"),
        P("fsdp", "tp"),
        P("tp", "fsdp"),
        P("fsdp"),
        P("fsdp", None),
        P(None, "fsdp", "tp"),
        P(None, "fsdp", "tp"),
        P(None, "tp", "fsdp"),
        P("fsdp", "ctx", None),
    )
    return jax.shard_map(
        body,
        mesh=mesh,
        in_specs=placed,
        out_specs=(
            P("fsdp", "ctx", None),
            P("fsdp", "ctx", None),
            P("fsdp"),
            P("fsdp", "tp"),
            P("fsdp", "tp"),
            P("fsdp", "tp"),
            P("tp", "fsdp"),
            P("fsdp"),
            P("fsdp", None),
            P(None, "fsdp", "tp"),
            P(None, "fsdp", "tp"),
            P(None, "tp", "fsdp"),
        ),
        check_vma=False,
    )
```

```python
import jax
import jax.numpy as jnp
from jax import lax
from jax.sharding import PartitionSpec as P

HD = 64
E = 32
TOPK = 8


epsilon = 1e-05
rope_base = 10000.0
masked_fill = -1e30


def matmul(left, right):
    return jnp.dot(left, right, preferred_element_type=jnp.float32)


def contract_rows(left, right):
    return lax.dot_general(
        left, right, (((0,), (0,)), ((), ())), preferred_element_type=jnp.float32
    )


def contract_cols(left, right):
    return lax.dot_general(
        left, right, (((1,), (1,)), ((), ())), preferred_element_type=jnp.float32
    )


def rms_factor(values):
    return lax.rsqrt(jnp.mean(values * values, axis=-1, keepdims=True) + epsilon)


def doc_positions(segments):
    index = lax.broadcasted_iota(jnp.int32, segments.shape, 1)
    earlier = jnp.concatenate([segments[:, :1], segments[:, :-1]], axis=1)
    starts = jnp.where((segments != earlier) | (index == 0), index, 0)
    return index - lax.cummax(starts, axis=1)


def rotary_tables(positions, head_size):
    half_size = head_size // 2
    exponent = jnp.arange(half_size, dtype=jnp.float32) * (-2.0 / head_size)
    angles = positions.astype(jnp.float32)[..., None] * jnp.power(rope_base, exponent)
    return (jnp.cos(angles), jnp.sin(angles))


def rotate(values, cosine, sine_tab):
    half_size = values.shape[-1] // 2
    first_half = values[..., :half_size]
    second_half = values[..., half_size:]
    cos_wide = cosine[..., None, :]
    sin_wide = sine_tab[..., None, :]
    return jnp.concatenate(
        [
            first_half * cos_wide - second_half * sin_wide,
            second_half * cos_wide + first_half * sin_wide,
        ],
        axis=-1,
    )


def norm_backward(grad_normed, normed, factor, gain):
    scaled = grad_normed * gain
    return factor * (scaled - normed * jnp.mean(scaled * normed, axis=-1, keepdims=True))


def column_pack(shards, groups):
    experts, depth, units = shards.shape
    local = experts // groups
    return (
        shards.reshape(groups, local, depth, units)
        .transpose(0, 2, 1, 3)
        .reshape(groups, depth, local * units)
    )


def column_unpack(packed, units):
    groups, depth, columns = packed.shape
    local = columns // units
    return (
        packed.reshape(groups, depth, local, units)
        .transpose(0, 2, 1, 3)
        .reshape(groups * local, depth, units)
    )


def gather_experts(shards, groups, ctx_count):
    packed = column_pack(shards, groups)
    part = packed.shape[2] // ctx_count
    mine = lax.dynamic_slice_in_dim(packed, lax.axis_index("ctx") * part, part, 2)
    moved = lax.all_to_all(mine, "fsdp", split_axis=0, concat_axis=0, tiled=True)
    return lax.all_gather(moved.reshape(-1, part), "ctx", axis=1, tiled=True)


def return_experts(grad, groups, units):
    summed = lax.psum_scatter(
        grad, "ctx", scatter_dimension=1, tiled=True
    )
    depth = summed.shape[0] // groups
    moved = lax.all_to_all(
        summed.reshape(groups, depth, -1), "fsdp", split_axis=0, concat_axis=0, tiled=True
    )
    return column_unpack(lax.all_gather(moved, "ctx", axis=2, tiled=True), units)


def router_probs(normed, router_w):
    logits = matmul(normed, router_w)
    exp_logits = jnp.exp(logits - jnp.max(logits, axis=-1, keepdims=True))
    return exp_logits / jnp.sum(exp_logits, axis=-1, keepdims=True)


def body(
    hidden_in,
    segment_ids,
    expert_ids,
    norm1_gain,
    w_query,
    w_key,
    w_value,
    w_output,
    norm2_gain,
    w_router,
    w_gate,
    w_up,
    w_down,
    cotangent,
):
    row_count, ctx_tok, model_width = hidden_in.shape
    tok_count = row_count * ctx_tok
    seq_len = segment_ids.shape[1]
    first_pos = lax.axis_index("ctx") * ctx_tok
    score_scale = HD ** (-0.5)
    groups = lax.axis_size("fsdp")
    ctx_count = lax.axis_size("ctx")
    hidden_units = w_gate.shape[2]
    q_cols, k_cols, o_cols = w_query.shape[1], w_key.shape[1], w_output.shape[0]
    small_at = q_cols + 2 * k_cols + o_cols
    shard_rows = w_query.shape[0]
    token_ids = expert_ids.reshape(tok_count, TOPK)
    route_mask = jnp.sum(
        (token_ids[:, :, None] == jnp.arange(E, dtype=jnp.int32)).astype(jnp.float32), axis=1
    )
    packed_w = lax.all_gather(
        jnp.concatenate(
            [
                w_query,
                w_key,
                w_value,
                w_output.T,
                w_router,
                norm1_gain[:, None],
                norm2_gain[:, None],
                jnp.zeros((shard_rows, 128 - E - 2), jnp.bfloat16),
                route_mask.astype(jnp.bfloat16).reshape(shard_rows, -1),
            ],
            axis=1,
        ),
        "fsdp",
        axis=0,
        tiled=True,
    )
    query_w = packed_w[:, :q_cols]
    key_w = packed_w[:, q_cols : q_cols + k_cols]
    value_w = packed_w[:, q_cols + k_cols : q_cols + 2 * k_cols]
    out_wt = packed_w[:, q_cols + 2 * k_cols : small_at]
    router_w = packed_w[:, small_at : small_at + E]
    gain_one = packed_w[:, small_at + E]
    gain_two = packed_w[:, small_at + E + 1]
    mask_all = packed_w[:, small_at + 128 :].reshape(-1, E)
    grad_all = lax.all_gather(
        cotangent.reshape(tok_count, model_width), "fsdp", axis=0, tiled=True
    )
    down_wt = gather_experts(w_down.transpose(0, 2, 1), groups, ctx_count)
    gate_w = gather_experts(w_gate, groups, ctx_count)
    up_w = gather_experts(w_up, groups, ctx_count)
    inputs = hidden_in.reshape(tok_count, model_width).astype(jnp.float32)
    factor_one = rms_factor(inputs)
    normed_one = inputs * factor_one
    first_in = (normed_one * gain_one.astype(jnp.float32)).astype(jnp.bfloat16)
    query_lin = matmul(first_in, query_w)
    key_lin = matmul(first_in, key_w)
    values = matmul(first_in, value_w).astype(jnp.bfloat16)
    heads_q = query_lin.shape[1] // HD
    heads_k = key_lin.shape[1] // HD
    group_size = heads_q // heads_k
    positions = doc_positions(segment_ids)
    local_pos = lax.dynamic_slice_in_dim(positions, first_pos, ctx_tok, 1).reshape(tok_count)
    cosine, sine_tab = rotary_tables(local_pos, HD)
    queries = rotate(query_lin.reshape(tok_count, heads_q, HD), cosine, sine_tab).astype(
        jnp.bfloat16
    )
    keys_rot = rotate(key_lin.reshape(tok_count, heads_k, HD), cosine, sine_tab).astype(
        jnp.bfloat16
    )
    kv_all = lax.all_gather(
        jnp.concatenate([keys_rot.reshape(tok_count, heads_k * HD), values], axis=1).reshape(
            row_count, ctx_tok, 2 * heads_k * HD
        ),
        "ctx",
        axis=1,
        tiled=True,
    )
    keys_all, values_all = kv_all[..., : heads_k * HD], kv_all[..., heads_k * HD :]
    pair_count = row_count * heads_k
    query_pairs = (
        queries.reshape(row_count, ctx_tok, heads_k, group_size, HD)
        .transpose(0, 2, 3, 1, 4)
        .reshape(pair_count, group_size * ctx_tok, HD)
    )
    key_pairs = (
        keys_all.reshape(row_count, seq_len, heads_k, HD)
        .transpose(0, 2, 1, 3)
        .reshape(pair_count, seq_len, HD)
    )
    value_pairs = (
        values_all.reshape(row_count, seq_len, heads_k, HD)
        .transpose(0, 2, 1, 3)
        .reshape(pair_count, seq_len, HD)
    )
    row_of = jnp.arange(pair_count, dtype=jnp.int32) // heads_k
    key_index = jnp.arange(seq_len, dtype=jnp.int32)
    query_index = jnp.tile(first_pos + jnp.arange(ctx_tok, dtype=jnp.int32), group_size)

    def pair_scores(query_block, key_block, row_pick):
        seg_row = lax.dynamic_index_in_dim(segment_ids, row_pick, 0, keepdims=False)
        seg_query = jnp.tile(lax.dynamic_slice_in_dim(seg_row, first_pos, ctx_tok), group_size)
        allowed = (key_index[None, :] <= query_index[:, None]) & (
            seg_query[:, None] == seg_row[None, :]
        )
        raw_scores = contract_cols(query_block, key_block) * score_scale
        return jnp.where(allowed, raw_scores, masked_fill)

    def forward_pair(parts_in):
        query_block, key_block, value_block, row_pick = parts_in
        scores = pair_scores(query_block, key_block, row_pick)
        row_max = jnp.max(scores, axis=-1, keepdims=True)
        exp_vals = jnp.exp(scores - row_max)
        totals = jnp.sum(exp_vals, axis=-1, keepdims=True)
        weights_p = (exp_vals / totals).astype(jnp.bfloat16)
        return (matmul(weights_p, value_block), (row_max + jnp.log(totals))[:, 0])

    mixture, log_totals = lax.map(forward_pair, (query_pairs, key_pairs, value_pairs, row_of))
    att_out = (
        mixture.reshape(row_count, heads_k, group_size, ctx_tok, HD)
        .transpose(0, 3, 1, 2, 4)
        .reshape(tok_count, heads_q * HD)
        .astype(jnp.bfloat16)
    )
    resid = inputs + lax.psum(
        contract_cols(att_out, out_wt).astype(jnp.bfloat16), "tp"
    ).astype(jnp.float32)
    factor_two = rms_factor(resid)
    normed_two = resid * factor_two
    second_in = (normed_two * gain_two.astype(jnp.float32)).astype(jnp.bfloat16)
    router = router_probs(second_in, router_w)
    ready_in = lax.optimization_barrier((second_in, grad_all, down_wt, gate_w, up_w))[0]
    normed_all = lax.all_gather(ready_in, "fsdp", axis=0, tiled=True)
    columns = gate_w.shape[1]
    column_expert = lax.axis_index("fsdp") * (columns // hidden_units) + (
        jnp.arange(columns, dtype=jnp.int32) // hidden_units
    )
    owner = (jnp.arange(E, dtype=jnp.int32)[:, None] == column_expert[None, :]).astype(
        jnp.float32
    )
    grad_mid = matmul(grad_all, down_wt)
    gates_all = router_probs(normed_all, router_w) * mask_all.astype(jnp.float32)
    gate_cols = jnp.dot(
        gates_all, owner, precision=lax.Precision.HIGHEST, preferred_element_type=jnp.float32
    )
    gate_pre = matmul(normed_all, gate_w)
    up_pre = matmul(normed_all, up_w)
    sigmoid_g = jax.nn.sigmoid(gate_pre)
    activated = gate_pre * sigmoid_g
    hidden = activated * up_pre
    weighted = (hidden * gate_cols).astype(jnp.bfloat16)
    grad_hidden = grad_mid * gate_cols
    grad_gate_pre = (
        grad_hidden * up_pre * sigmoid_g * (1.0 + gate_pre * (1.0 - sigmoid_g))
    ).astype(jnp.bfloat16)
    grad_up_pre = (grad_hidden * activated).astype(jnp.bfloat16)
    gate_grad_all = contract_cols(
        (hidden * grad_mid).astype(jnp.bfloat16), owner.astype(jnp.bfloat16)
    )
    grad_rows = contract_cols(grad_gate_pre, gate_w) + contract_cols(grad_up_pre, up_w)
    arrived = lax.psum_scatter(
        jnp.concatenate(
            [
                grad_rows.astype(jnp.bfloat16),
                gate_grad_all.astype(jnp.bfloat16),
                jnp.zeros((grad_rows.shape[0], 128 - E), jnp.bfloat16),
            ],
            axis=1,
        ),
        "fsdp",
        scatter_dimension=0,
        tiled=True,
    )
    gate_grad_w = contract_rows(normed_all, grad_gate_pre).astype(jnp.bfloat16)
    up_grad_w = contract_rows(normed_all, grad_up_pre).astype(jnp.bfloat16)
    down_grad_w = contract_rows(grad_all, weighted).astype(jnp.bfloat16)
    moe_made = contract_cols(weighted, down_wt).astype(jnp.bfloat16)
    moe_rows = lax.optimization_barrier((moe_made, arrived))[0]
    settled = lax.optimization_barrier(
        (arrived, gate_grad_w, up_grad_w, down_grad_w, moe_made)
    )[0]
    grad_in_part = settled[:, :model_width]
    grad_route = settled[:, model_width : model_width + E].astype(jnp.float32) * route_mask
    moe_part = lax.psum_scatter(moe_rows, "fsdp", scatter_dimension=0, tiled=True)
    gate_part = return_experts(gate_grad_w, groups, hidden_units)
    up_part = return_experts(up_grad_w, groups, hidden_units)
    down_part = return_experts(down_grad_w, groups, hidden_units).transpose(0, 2, 1)
    grad_out = cotangent.reshape(tok_count, model_width).astype(jnp.float32)
    grad_logits = (
        router * (grad_route - jnp.sum(router * grad_route, axis=-1, keepdims=True))
    ).astype(jnp.bfloat16)
    grad_router = contract_rows(second_in, grad_logits)
    grad_second = lax.psum(
        (grad_in_part.astype(jnp.float32) + contract_cols(grad_logits, router_w)).astype(
            jnp.bfloat16
        ),
        "tp",
    ).astype(jnp.float32)
    moe_part, _ = lax.optimization_barrier((moe_part, grad_second))
    moe_total = lax.psum(moe_part, "tp").astype(jnp.float32)
    block_out = (resid + moe_total).astype(jnp.bfloat16).reshape(row_count, ctx_tok, model_width)
    grad_gain_two = jnp.sum(grad_second * normed_two, axis=0)
    grad_resid = grad_out + norm_backward(
        grad_second, normed_two, factor_two, gain_two.astype(jnp.float32)
    )
    grad_att = grad_resid.astype(jnp.bfloat16)
    grad_out_wt = contract_rows(grad_att, att_out)
    grad_att_out = matmul(grad_att, out_wt).astype(jnp.bfloat16)
    grad_out_pairs = (
        grad_att_out.reshape(row_count, ctx_tok, heads_k, group_size, HD)
        .transpose(0, 2, 3, 1, 4)
        .reshape(pair_count, group_size * ctx_tok, HD)
    )

    def backward_pair(parts_in):
        query_block, key_block, value_block, grad_block, log_row, row_pick = parts_in
        scores = pair_scores(query_block, key_block, row_pick)
        weights_p = jnp.exp(scores - log_row[:, None])
        grad_p = contract_cols(grad_block, value_block)
        grad_v = contract_rows(weights_p.astype(jnp.bfloat16), grad_block)
        grad_s = (
            weights_p * (grad_p - jnp.sum(weights_p * grad_p, axis=-1, keepdims=True))
        ).astype(jnp.bfloat16)
        grad_q = matmul(grad_s, key_block) * score_scale
        grad_k = contract_rows(grad_s, query_block) * score_scale
        return (grad_q, grad_k, grad_v)

    grad_q_pairs, grad_k_pairs, grad_v_pairs = lax.map(
        backward_pair, (query_pairs, key_pairs, value_pairs, grad_out_pairs, log_totals, row_of)
    )
    grad_k_rows = (
        grad_k_pairs.reshape(row_count, heads_k, seq_len, HD)
        .transpose(0, 2, 1, 3)
        .reshape(row_count, seq_len, heads_k * HD)
    )
    grad_v_rows = (
        grad_v_pairs.reshape(row_count, heads_k, seq_len, HD)
        .transpose(0, 2, 1, 3)
        .reshape(row_count, seq_len, heads_k * HD)
    )
    own_kv = lax.psum_scatter(
        jnp.concatenate([grad_k_rows, grad_v_rows], axis=2).astype(jnp.bfloat16),
        "ctx",
        scatter_dimension=1,
        tiled=True,
    ).astype(jnp.float32)
    own_k, own_v = own_kv[..., : heads_k * HD], own_kv[..., heads_k * HD :]
    grad_q_rot = (
        grad_q_pairs.reshape(row_count, heads_k, group_size, ctx_tok, HD)
        .transpose(0, 3, 1, 2, 4)
        .reshape(tok_count, heads_q, HD)
    )
    grad_query_lin = (
        rotate(grad_q_rot, cosine, -sine_tab).reshape(tok_count, heads_q * HD).astype(jnp.bfloat16)
    )
    grad_key_lin = (
        rotate(own_k.reshape(tok_count, heads_k, HD), cosine, -sine_tab)
        .reshape(tok_count, heads_k * HD)
        .astype(jnp.bfloat16)
    )
    grad_value_lin = own_v.reshape(tok_count, heads_k * HD).astype(jnp.bfloat16)
    grad_qkv = contract_rows(
        first_in, jnp.concatenate([grad_query_lin, grad_key_lin, grad_value_lin], axis=1)
    )
    grad_first_part = (
        contract_cols(grad_query_lin, query_w)
        + contract_cols(grad_key_lin, key_w)
        + contract_cols(grad_value_lin, value_w)
    )
    grad_first_part, _ = lax.optimization_barrier((grad_first_part, moe_total))
    grad_first = lax.psum(grad_first_part.astype(jnp.bfloat16), "tp").astype(jnp.float32)
    grad_input = grad_resid + norm_backward(
        grad_first, normed_one, factor_one, gain_one.astype(jnp.float32)
    )
    grad_gain_one = jnp.sum(grad_first_part * normed_one, axis=0)
    counted = (lax.axis_index("tp") == 0).astype(jnp.float32)
    dense = lax.psum_scatter(
        jnp.concatenate(
            [
                grad_qkv.astype(jnp.bfloat16),
                grad_out_wt.astype(jnp.bfloat16),
                grad_router.astype(jnp.bfloat16),
                grad_gain_one.astype(jnp.bfloat16)[:, None],
                (grad_gain_two * counted).astype(jnp.bfloat16)[:, None],
                jnp.zeros((model_width, 128 - E - 2), jnp.bfloat16),
            ],
            axis=1,
        ),
        "fsdp",
        scatter_dimension=0,
        tiled=True,
    )
    large = lax.psum(dense[:, :small_at], "ctx").astype(jnp.float32)
    small = lax.psum(dense[:, small_at:], ("ctx", "tp")).astype(jnp.float32)
    return (
        block_out,
        grad_input.reshape(row_count, ctx_tok, model_width),
        small[:, E],
        large[:, :q_cols],
        large[:, q_cols : q_cols + k_cols],
        large[:, q_cols + k_cols : q_cols + 2 * k_cols],
        large[:, q_cols + 2 * k_cols :].T,
        small[:, E + 1],
        small[:, :E],
        gate_part.astype(jnp.float32),
        up_part.astype(jnp.float32),
        down_part.astype(jnp.float32),
    )


def solution(mesh):
    placed = (
        P("fsdp", "ctx", None),
        P("fsdp", None),
        P("fsdp", "ctx", None),
        P("fsdp"),
        P("fsdp", "tp"),
        P("fsdp", "tp"),
        P("fsdp", "tp"),
        P("tp", "fsdp"),
        P("fsdp"),
        P("fsdp", None),
        P(None, "fsdp", "tp"),
        P(None, "fsdp", "tp"),
        P(None, "tp", "fsdp"),
        P("fsdp", "ctx", None),
    )
    return jax.shard_map(
        body,
        mesh=mesh,
        in_specs=placed,
        out_specs=(
            P("fsdp", "ctx", None),
            P("fsdp", "ctx", None),
            P("fsdp"),
            P("fsdp", "tp"),
            P("fsdp", "tp"),
            P("fsdp", "tp"),
            P("tp", "fsdp"),
            P("fsdp"),
            P("fsdp", None),
            P(None, "fsdp", "tp"),
            P(None, "fsdp", "tp"),
            P(None, "tp", "fsdp"),
        ),
        check_vma=False,
    )
```
